32 devices in a mesh: row: 8 (over z, x), col: 4 (over y, core).
Axes of the slice: x: 2, y: 2, z: 4, core: 2. Of those that a mesh axis runs over, the one named last changes fastest.
Arguments:
- rhs: bfloat16 [32768, 256], P(('row', 'col')), may hold values from -6 to 6
- order: int32 [32, 1024], P(('row', 'col')), may hold values from 0 to 1023, each once within a row
- leaf_inverse: bfloat16 [64, 512, 512], P(('row', 'col')), may hold values from -1 to 2
- leaf_column_generator: bfloat16 [64, 512, 256], P(('row', 'col')), may hold values from -0.25 to 0.25
- factor_up: bfloat16 [32, 5, 256, 256], P(('row', 'col')), may hold values from -1 to 1
- downward_coupling_factors: bfloat16 [32, 5, 256, 256], P(('row', 'col')), may hold values from -1 to 2
Outputs:
- solution: bfloat16 [32768, 256], P(('row', 'col'))
The draws below stay inside these ranges and needn't reach their ends.
All inputs are finite; a program needn't handle non-finite values.
Results may differ from the reference program's by a relative error of at most 0.015.
Values may be sent and summed in bfloat16 or wider, within the bound.
A program may use at most 64 MiB of HBM per device.

```python
import math
import jax
import jax.numpy as jnp
import numpy as np
from jax import lax

R = 256
G = 256
LEAF = 512
LEAVES_DEV = 2
LEVELS = 5
BINS_DEV = 1024
BINS = 32768
LEAVES = 64
N_ROW = 8
N_COL = 4


def draw_leaf_inverse(key, part):
    shape = (LEAVES_DEV * N_ROW * N_COL, LEAF, LEAF)
    noise = jnp.clip(jax.random.normal(jax.random.fold_in(key, 21), shape, jnp.float32), -4.0, 4.0)
    diagonal_block = jnp.ones(shape[:-1], jnp.float32)
    eye = jnp.eye(LEAF, dtype=jnp.float32)
    return (diagonal_block[..., None] * eye + 0.5 * noise / math.sqrt(LEAF)).astype(jnp.bfloat16)


def draw_factor_up(key, part):
    shape = (N_ROW * N_COL, LEVELS, R, R)
    noise = jnp.clip(jax.random.normal(jax.random.fold_in(key, 31), shape, jnp.float32), -4.0, 4.0)
    diagonal_block = jnp.full(shape[:-1], 0.6, jnp.float32)
    eye = jnp.eye(R, dtype=jnp.float32)
    return (diagonal_block[..., None] * eye + 0.37 * noise / math.sqrt(R)).astype(jnp.bfloat16)


def draw_downward_coupling_factors(key, part):
    shape = (N_ROW * N_COL, LEVELS, R, R)
    noise = jnp.clip(jax.random.normal(jax.random.fold_in(key, 41), shape, jnp.float32), -4.0, 4.0)
    diagonal_block = jnp.full(shape[:-1], 1.2, jnp.float32)
    eye = jnp.eye(R, dtype=jnp.float32)
    return (diagonal_block[..., None] * eye + 0.37 * noise / math.sqrt(R)).astype(jnp.bfloat16)


def shard_levels(stream_key, extent, cuts, smallest, largest):
    loudness = 1.0
    for dim, shards_of in cuts:
        steps = jax.random.uniform(jax.random.fold_in(jax.random.fold_in(stream_key, 6), dim), (shards_of,), jnp.float32, smallest / len(cuts), largest / len(cuts))
        loudness = loudness * jnp.repeat(jnp.exp(steps), extent[dim] // shards_of).reshape((-1,) + (1,) * (len(extent) - 1 - dim))
    return loudness


def gaussian(rng, dims, width, limit, shards=(), kind=jnp.bfloat16):
    gain = shard_levels(rng, dims, shards, -0.22, 0.18) if shards else 1.0
    result = jax.random.normal(rng, dims, jnp.float32) * width * gain
    return jnp.minimum(jnp.maximum(result, -limit), limit).astype(kind)


def setup_inputs(seed: int = 0) -> dict:
    key_list = jax.random.split(jax.random.key(seed), 7)
    rhs = gaussian(key_list[0], (BINS, G), 1.0, 6.0, ((0, 32),))
    order = jax.vmap(lambda own: jax.random.permutation(own, BINS_DEV))(jax.random.split(key_list[1], (N_ROW * N_COL))).reshape((N_ROW * N_COL, BINS_DEV)).astype(jnp.int32)
    leaf_inverse = draw_leaf_inverse(jax.random.fold_in(key_list[6], 71), 0)
    leaf_column_generator = gaussian(key_list[3], (LEAVES, LEAF, R), LEAF ** -0.5, 0.25, ((0, 32),))
    factor_up = draw_factor_up(jax.random.fold_in(key_list[6], 71), 0)
    downward_coupling_factors = draw_downward_coupling_factors(jax.random.fold_in(key_list[6], 71), 0)
    return dict(rhs=rhs, order=order, leaf_inverse=leaf_inverse, leaf_column_generator=leaf_column_generator, factor_up=factor_up, downward_coupling_factors=downward_coupling_factors)


def leaf_section(pieces):
    blocks, inverse, basis = pieces
    eliminated_rows = jnp.einsum('jab,jbg->jag', inverse.astype(jnp.float32), blocks.astype(jnp.float32))
    rounded = lax.optimization_barrier(eliminated_rows.astype(jnp.bfloat16)).astype(jnp.float32)
    solve_state = jnp.einsum('dmq,dms->qs', basis.astype(jnp.float32), rounded)
    return eliminated_rows, solve_state


def finish_section(pieces):
    eliminated_rows, top, inverse, basis, positions = pieces
    top_half = lax.optimization_barrier(top.astype(jnp.bfloat16)).astype(jnp.float32)
    back = jnp.einsum('jar,rg->jag', basis.astype(jnp.float32), top_half)
    back_half = lax.optimization_barrier(back.astype(jnp.bfloat16)).astype(jnp.float32)
    solved = eliminated_rows - jnp.einsum('jab,jbg->jag', inverse.astype(jnp.float32), back_half)
    flat = solved.reshape(BINS_DEV, G).astype(jnp.bfloat16)
    placed = jnp.zeros((BINS_DEV, G), jnp.bfloat16)
    return placed.at[positions].set(flat)


def reference(rhs, order, leaf_inverse, leaf_column_generator, factor_up, downward_coupling_factors):
    devices = N_ROW * N_COL
    grouped = rhs.reshape(devices, BINS_DEV, G)
    ordered = jnp.take_along_axis(grouped, order[:, :, None], axis=1)
    blocks = ordered.reshape(devices, LEAVES_DEV, LEAF, G)
    inverse = leaf_inverse.reshape(devices, LEAVES_DEV, LEAF, LEAF)
    basis = leaf_column_generator.reshape(devices, LEAVES_DEV, LEAF, R)
    eliminated_rows, solve_state = lax.map(leaf_section, (blocks, inverse, basis))
    saved = []
    for level in range(LEVELS):
        partner = np.arange(devices) ^ (1 << level)
        saved.append(solve_state)
        rounded = lax.optimization_barrier(solve_state.astype(jnp.bfloat16)).astype(jnp.float32)
        term = jnp.einsum('dij,djg->dig', factor_up[:, level].astype(jnp.float32), rounded)
        term_half = lax.optimization_barrier(term.astype(jnp.bfloat16)).astype(jnp.float32)
        solve_state = term_half + term_half[partner]
    top = solve_state
    for level in reversed(range(LEVELS)):
        partner = np.arange(devices) ^ (1 << level)
        rounded = lax.optimization_barrier(top.astype(jnp.bfloat16)).astype(jnp.float32)
        own = jnp.einsum('dji,djg->dig', factor_up[:, level].astype(jnp.float32), rounded)
        sent = jnp.einsum('dij,djg->dig', downward_coupling_factors[:, level].astype(jnp.float32), rounded)
        sent_half = lax.optimization_barrier(sent.astype(jnp.bfloat16)).astype(jnp.float32)
        top = saved[level] + 0.5 * (sent_half[partner] - own)
    placed = lax.map(finish_section, (eliminated_rows, top, inverse, basis, order))
    return placed.reshape(BINS, G)
```

```python
import functools

import jax
import jax.numpy as jnp
from jax import lax
from jax.experimental import pallas as pl
from jax.experimental.pallas import tpu as pltpu
from jax.sharding import PartitionSpec as P

CHUNKS = 4
LEAF_PARTS = 2


def nn(a, b):
    return lax.dot_general(a, b, (((1,), (0,)), ((), ())), preferred_element_type=jnp.float32)


def nt(a, b):
    return lax.dot_general(a, b, (((1,), (1,)), ((), ())), preferred_element_type=jnp.float32)


def flipped(index, bit):
    return index + bit * (1 - 2 * lax.rem(lax.div(index, bit), 2))


def kernel(
    col_bits,
    chunks,
    leaf_parts,
    order_ref,
    rhs_ref,
    inv_ref,
    gen_ref,
    up_ref,
    down_ref,
    out_ref,
    rhs_v,
    inv_v,
    gen_v,
    up_v,
    down_v,
    far_v,
    place,
    elim,
    states,
    flat,
    send,
    recv,
    load_sem,
    send_sem,
    recv_sem,
    far_sem,
):
    bf16, f32 = jnp.bfloat16, jnp.float32
    levels = up_v.shape[0]
    leaves, leaf, _ = inv_v.shape
    bins, genes = rhs_v.shape
    piece = genes // chunks
    row, col = lax.axis_index("row"), lax.axis_index("col")
    partners = []
    for level in range(levels):
        if level < col_bits:
            partners.append((row, flipped(col, 1 << level)))
        else:
            partners.append((flipped(row, 1 << (level - col_bits)), col))

    barrier = pltpu.get_barrier_semaphore()
    for partner in partners:
        pl.semaphore_signal(
            barrier, inc=1, device_id=partner, device_id_type=pl.DeviceIdType.MESH
        )

    loads = [
        pltpu.make_async_copy(source, target, load_sem.at[i])
        for i, (source, target) in enumerate(
            ((rhs_ref, rhs_v), (inv_ref, inv_v), (gen_ref, gen_v), (up_ref.at[0], up_v),
             (down_ref.at[0], down_v))
        )
    ]
    for load in loads:
        load.start()

    block = 128
    for start in range(0, bins, block):
        index = lax.broadcasted_iota(jnp.int32, (block, bins), 0) + start
        hit = index == order_ref[...]
        place[start : start + block, :] = jnp.where(hit, 1.0, 0.0).astype(bf16)

    pl.semaphore_wait(barrier, levels)

    far = pltpu.make_async_remote_copy(
        src_ref=down_ref.at[0, levels - 1],
        dst_ref=far_v,
        send_sem=far_sem.at[0],
        recv_sem=far_sem.at[1],
        device_id=partners[levels - 1],
        device_id_type=pl.DeviceIdType.MESH,
    )
    far.start()

    events = list(range(levels)) + list(reversed(range(levels - 1)))
    copies = {}

    def rows(c):
        return slice(c * piece, (c + 1) * piece)

    def start(event, c, value):
        send[event, rows(c), :] = value
        copy = pltpu.make_async_remote_copy(
            src_ref=send.at[event, pl.ds(c * piece, piece)],
            dst_ref=recv.at[event, pl.ds(c * piece, piece)],
            send_sem=send_sem.at[event, c],
            recv_sem=recv_sem.at[event, c],
            device_id=partners[events[event]],
            device_id_type=pl.DeviceIdType.MESH,
        )
        copy.start()
        copies[event, c] = copy

    part = genes // leaf_parts
    loads[0].wait()
    rhs_t = rhs_v[...].T
    for h in range(leaf_parts):
        span = slice(h * part, (h + 1) * part)
        state = None
        for j in range(leaves):
            ordered = nn(rhs_t[span, :], place[:, j * leaf : (j + 1) * leaf]).astype(bf16)
            if h == 0 and j == 0:
                loads[1].wait()
            value = nt(ordered, inv_v[j])
            elim[j, span, :] = value
            if h == 0 and j == 0:
                loads[2].wait()
            own = nn(value.astype(bf16), gen_v[j])
            state = own if state is None else state + own
        states[0, span, :] = state
        if h == 0:
            loads[3].wait()
        term = nt(state.astype(bf16), up_v[0]).astype(bf16)
        for c in range(chunks // leaf_parts):
            start(0, h * (chunks // leaf_parts) + c, term[c * piece : (c + 1) * piece, :])

    for level in range(1, levels):
        for c in range(chunks):
            copies[level - 1, c].wait_recv()
            state = send[level - 1, rows(c), :].astype(f32) + recv[level - 1, rows(c), :].astype(
                f32
            )
            states[level, rows(c), :] = state
            start(level, c, nt(state.astype(bf16), up_v[level]).astype(bf16))

    for event in range(levels, 2 * levels - 1):
        level = events[event]
        for c in range(chunks):
            copies[event - 1, c].wait_recv()
            came = recv[event - 1, rows(c), :].astype(f32)
            if event == levels:
                if c == 0:
                    loads[4].wait()
                    far.wait_recv()
                y = (send[event - 1, rows(c), :].astype(f32) + came).astype(bf16)
                coupled = nt(y, far_v[...]).astype(bf16).astype(f32)
                top = states[levels - 1, rows(c), :] + 0.5 * (coupled - nn(y, up_v[levels - 1]))
            else:
                top = states[level + 1, rows(c), :] + 0.5 * came
            y = top.astype(bf16)
            start(event, c, nt(y, down_v[level]).astype(bf16))
            states[level, rows(c), :] = states[level, rows(c), :] - 0.5 * nn(y, up_v[level])

    last = 2 * levels - 2
    for c in range(chunks):
        copies[last, c].wait_recv()
        top = states[0, rows(c), :] + 0.5 * recv[last, rows(c), :].astype(f32)
        y = top.astype(bf16)
        for j in range(leaves):
            back = nt(y, gen_v[j]).astype(bf16)
            solved = elim[j, rows(c), :] - nt(back, inv_v[j])
            flat[rows(c), j * leaf : (j + 1) * leaf] = solved.astype(bf16)
    out_ref[...] = nt(place[...], flat[...]).astype(bf16)

    for copy in copies.values():
        copy.wait_send()
    far.wait_send()


def on_device(
    rhs, order, leaf_inverse, leaf_column_generator, factor_up, downward_coupling_factors
):
    leaves, leaf, _ = leaf_inverse.shape
    rank = leaf_column_generator.shape[2]
    bins, genes = rhs.shape
    levels = factor_up.shape[1]
    col_bits = lax.axis_size("col").bit_length() - 1
    bf16, f32 = jnp.bfloat16, jnp.float32
    exchanges = 2 * levels - 1
    return pl.pallas_call(
        functools.partial(kernel, col_bits, CHUNKS, LEAF_PARTS),
        out_shape=jax.ShapeDtypeStruct((bins, genes), bf16),
        in_specs=[pl.BlockSpec(memory_space=pltpu.VMEM)] + [pl.BlockSpec(memory_space=pl.ANY)] * 5,
        out_specs=pl.BlockSpec(memory_space=pltpu.VMEM),
        scratch_shapes=[
            pltpu.VMEM((bins, genes), bf16),
            pltpu.VMEM((leaves, leaf, leaf), bf16),
            pltpu.VMEM((leaves, leaf, rank), bf16),
            pltpu.VMEM((levels, rank, rank), bf16),
            pltpu.VMEM((levels, rank, rank), bf16),
            pltpu.VMEM((rank, rank), bf16),
            pltpu.VMEM((bins, bins), bf16),
            pltpu.VMEM((leaves, genes, leaf), f32),
            pltpu.VMEM((levels, genes, rank), f32),
            pltpu.VMEM((genes, bins), bf16),
            pltpu.VMEM((exchanges, genes, rank), bf16),
            pltpu.VMEM((exchanges, genes, rank), bf16),
            pltpu.SemaphoreType.DMA((5,)),
            pltpu.SemaphoreType.DMA((exchanges, CHUNKS)),
            pltpu.SemaphoreType.DMA((exchanges, CHUNKS)),
            pltpu.SemaphoreType.DMA((2,)),
        ],
        compiler_params=pltpu.CompilerParams(
            collective_id=0, has_side_effects=True, vmem_limit_bytes=48 * 1024 * 1024
        ),
        cost_estimate=pl.CostEstimate(
            flops=2 * (2 * bins * bins * genes + 2 * bins * leaf * genes + 2 * bins * rank * genes
                       + 3 * levels * rank * rank * genes),
            bytes_accessed=4 * bins * genes + 2 * leaves * leaf * (leaf + rank)
            + 4 * levels * rank * rank,
            transcendentals=0,
        ),
    )(order, rhs, leaf_inverse, leaf_column_generator, factor_up, downward_coupling_factors)


def solution(mesh):
    in_specs = (
        P(("row", "col"), None),
        P(("row", "col"), None),
        P(("row", "col"), None, None),
        P(("row", "col"), None, None),
        P(("row", "col"), None, None, None),
        P(("row", "col"), None, None, None),
    )
    out_specs = P(("row", "col"), None)
    return jax.shard_map(
        on_device, mesh=mesh, in_specs=in_specs, out_specs=out_specs, check_vma=False
    )
```

```python
import functools

import jax
import jax.numpy as jnp
from jax import lax
from jax.experimental import pallas as pl
from jax.experimental.pallas import tpu as pltpu
from jax.sharding import PartitionSpec as P

CHUNKS = 4
LEAF_PARTS = 2


def nn(a, b):
    return lax.dot_general(a, b, (((1,), (0,)), ((), ())), preferred_element_type=jnp.float32)


def nt(a, b):
    return lax.dot_general(a, b, (((1,), (1,)), ((), ())), preferred_element_type=jnp.float32)


def flipped(index, bit):
    return index + bit * (1 - 2 * lax.rem(lax.div(index, bit), 2))


def kernel(
    col_bits,
    chunks,
    leaf_parts,
    order_ref,
    rhs_ref,
    inv_ref,
    gen_ref,
    up_ref,
    down_ref,
    out_ref,
    order_v,
    rhs_v,
    inv_v,
    gen_v,
    up_v,
    down_v,
    far_v,
    place,
    elim,
    states,
    flat,
    ys,
    send,
    recv,
    load_sem,
    send_sem,
    recv_sem,
    far_sem,
):
    bf16, f32 = jnp.bfloat16, jnp.float32
    levels = up_v.shape[0]
    leaves, leaf, _ = inv_v.shape
    bins, genes = rhs_v.shape
    piece = genes // chunks
    row, col = lax.axis_index("row"), lax.axis_index("col")
    partners = []
    for level in range(levels):
        if level < col_bits:
            partners.append((row, flipped(col, 1 << level)))
        else:
            partners.append((flipped(row, 1 << (level - col_bits)), col))

    barrier = pltpu.get_barrier_semaphore()
    for partner in partners:
        pl.semaphore_signal(
            barrier, inc=1, device_id=partner, device_id_type=pl.DeviceIdType.MESH
        )

    loads = [
        pltpu.make_async_copy(source, target, load_sem.at[i])
        for i, (source, target) in enumerate(
            ((order_ref, order_v), (rhs_ref, rhs_v), (inv_ref, inv_v), (gen_ref, gen_v),
             (up_ref.at[0], up_v), (down_ref.at[0], down_v))
        )
    ]
    for load in loads:
        load.start()

    loads[0].wait()
    block = 128
    for start in range(0, bins, block):
        index = lax.broadcasted_iota(jnp.int32, (block, bins), 0) + start
        hit = index == order_v[...]
        place[start : start + block, :] = jnp.where(hit, 1.0, 0.0).astype(bf16)

    pl.semaphore_wait(barrier, levels)

    far = pltpu.make_async_remote_copy(
        src_ref=down_ref.at[0, levels - 1],
        dst_ref=far_v,
        send_sem=far_sem.at[0],
        recv_sem=far_sem.at[1],
        device_id=partners[levels - 1],
        device_id_type=pl.DeviceIdType.MESH,
    )
    far.start()

    events = list(range(levels)) + list(reversed(range(levels - 1)))
    copies = {}

    def rows(c):
        return slice(c * piece, (c + 1) * piece)

    def start(event, c, value):
        send[event, rows(c), :] = value
        copy = pltpu.make_async_remote_copy(
            src_ref=send.at[event, pl.ds(c * piece, piece)],
            dst_ref=recv.at[event, pl.ds(c * piece, piece)],
            send_sem=send_sem.at[event, c],
            recv_sem=recv_sem.at[event, c],
            device_id=partners[events[event]],
            device_id_type=pl.DeviceIdType.MESH,
        )
        copy.start()
        copies[event, c] = copy

    part = genes // leaf_parts
    loads[1].wait()
    rhs_t = rhs_v[...].T
    for h in range(leaf_parts):
        span = slice(h * part, (h + 1) * part)
        state = None
        for j in range(leaves):
            ordered = nn(rhs_t[span, :], place[:, j * leaf : (j + 1) * leaf]).astype(bf16)
            if h == 0 and j == 0:
                loads[2].wait()
            value = nt(ordered, inv_v[j])
            elim[j, span, :] = value
            if h == 0 and j == 0:
                loads[3].wait()
            own = nn(value.astype(bf16), gen_v[j])
            state = own if state is None else state + own
        states[0, span, :] = state
        if h == 0:
            loads[4].wait()
        term = nt(state.astype(bf16), up_v[0]).astype(bf16)
        for c in range(chunks // leaf_parts):
            start(0, h * (chunks // leaf_parts) + c, term[c * piece : (c + 1) * piece, :])

    for level in range(1, levels):
        for c in range(chunks):
            copies[level - 1, c].wait_recv()
            state = send[level - 1, rows(c), :].astype(f32) + recv[level - 1, rows(c), :].astype(
                f32
            )
            states[level, rows(c), :] = state
            start(level, c, nt(state.astype(bf16), up_v[level]).astype(bf16))

    for event in range(levels, 2 * levels - 1):
        level = events[event]
        for c in range(chunks):
            copies[event - 1, c].wait_recv()
            came = recv[event - 1, rows(c), :].astype(f32)
            if event == levels:
                if c == 0:
                    loads[5].wait()
                    far.wait_recv()
                y = (send[event - 1, rows(c), :].astype(f32) + came).astype(bf16)
                coupled = nt(y, far_v[...]).astype(bf16).astype(f32)
                top = states[levels - 1, rows(c), :] + 0.5 * (coupled - nn(y, up_v[levels - 1]))
            else:
                top = states[level + 1, rows(c), :] + 0.5 * came
            y = top.astype(bf16)
            start(event, c, nt(y, down_v[level]).astype(bf16))
            ys[rows(c), :] = y
        states[level] = states[level] - 0.5 * nn(ys[...], up_v[level])

    last = 2 * levels - 2
    for h in range(leaf_parts):
        span = slice(h * part, (h + 1) * part)
        for c in range(h * (chunks // leaf_parts), (h + 1) * (chunks // leaf_parts)):
            copies[last, c].wait_recv()
        top = states[0, span, :] + 0.5 * recv[last, span, :].astype(f32)
        y = top.astype(bf16)
        for j in range(leaves):
            back = nt(y, gen_v[j]).astype(bf16)
            solved = elim[j, span, :] - nt(back, inv_v[j])
            flat[span, j * leaf : (j + 1) * leaf] = solved.astype(bf16)
    out_ref[...] = nt(place[...], flat[...]).astype(bf16)

    for copy in copies.values():
        copy.wait_send()
    far.wait_send()


def on_device(
    rhs, order, leaf_inverse, leaf_column_generator, factor_up, downward_coupling_factors
):
    leaves, leaf, _ = leaf_inverse.shape
    rank = leaf_column_generator.shape[2]
    bins, genes = rhs.shape
    levels = factor_up.shape[1]
    col_bits = lax.axis_size("col").bit_length() - 1
    bf16, f32 = jnp.bfloat16, jnp.float32
    exchanges = 2 * levels - 1
    return pl.pallas_call(
        functools.partial(kernel, col_bits, CHUNKS, LEAF_PARTS),
        out_shape=jax.ShapeDtypeStruct((bins, genes), bf16),
        in_specs=[pl.BlockSpec(memory_space=pltpu.HBM)] * 6,
        out_specs=pl.BlockSpec(memory_space=pltpu.VMEM),
        scratch_shapes=[
            pltpu.VMEM((1, bins), jnp.int32),
            pltpu.VMEM((bins, genes), bf16),
            pltpu.VMEM((leaves, leaf, leaf), bf16),
            pltpu.VMEM((leaves, leaf, rank), bf16),
            pltpu.VMEM((levels, rank, rank), bf16),
            pltpu.VMEM((levels, rank, rank), bf16),
            pltpu.VMEM((rank, rank), bf16),
            pltpu.VMEM((bins, bins), bf16),
            pltpu.VMEM((leaves, genes, leaf), f32),
            pltpu.VMEM((levels, genes, rank), f32),
            pltpu.VMEM((genes, bins), bf16),
            pltpu.VMEM((genes, rank), bf16),
            pltpu.VMEM((exchanges, genes, rank), bf16),
            pltpu.VMEM((exchanges, genes, rank), bf16),
            pltpu.SemaphoreType.DMA((6,)),
            pltpu.SemaphoreType.DMA((exchanges, CHUNKS)),
            pltpu.SemaphoreType.DMA((exchanges, CHUNKS)),
            pltpu.SemaphoreType.DMA((2,)),
        ],
        compiler_params=pltpu.CompilerParams(
            collective_id=0, has_side_effects=True, vmem_limit_bytes=60 * 1024 * 1024
        ),
        cost_estimate=pl.CostEstimate(
            flops=2 * (2 * bins * bins * genes + 2 * bins * leaf * genes + 2 * bins * rank * genes
                       + 3 * levels * rank * rank * genes),
            bytes_accessed=4 * bins * genes + 2 * leaves * leaf * (leaf + rank)
            + 4 * levels * rank * rank,
            transcendentals=0,
        ),
    )(order, rhs, leaf_inverse, leaf_column_generator, factor_up, downward_coupling_factors)


def solution(mesh):
    in_specs = (
        P(("row", "col"), None),
        P(("row", "col"), None),
        P(("row", "col"), None, None),
        P(("row", "col"), None, None),
        P(("row", "col"), None, None, None),
        P(("row", "col"), None, None, None),
    )
    out_specs = P(("row", "col"), None)
    return jax.shard_map(
        on_device, mesh=mesh, in_specs=in_specs, out_specs=out_specs, check_vma=False
    )
```

```python
import functools

import jax
import jax.numpy as jnp
from jax import lax
from jax.experimental import pallas as pl
from jax.experimental.pallas import tpu as pltpu
from jax.sharding import PartitionSpec as P

CHUNKS = 4
LEAF_PARTS = 2


def nn(a, b):
    return lax.dot_general(a, b, (((1,), (0,)), ((), ())), preferred_element_type=jnp.float32)


def nt(a, b):
    return lax.dot_general(a, b, (((1,), (1,)), ((), ())), preferred_element_type=jnp.float32)


def flipped(index, bit):
    return index + bit * (1 - 2 * lax.rem(lax.div(index, bit), 2))


def kernel(
    col_bits,
    chunks,
    leaf_parts,
    order_ref,
    rhs_ref,
    inv_ref,
    gen_ref,
    up_ref,
    down_ref,
    out_ref,
    order_v,
    rhs_v,
    inv_v,
    gen_v,
    up_v,
    down_v,
    far_v,
    place,
    elim,
    states,
    flat,
    send,
    recv,
    load_sem,
    send_sem,
    recv_sem,
    far_sem,
):
    bf16, f32 = jnp.bfloat16, jnp.float32
    levels = up_v.shape[0]
    leaves, leaf, _ = inv_v.shape
    bins, genes = rhs_v.shape
    piece = genes // chunks
    row, col = lax.axis_index("row"), lax.axis_index("col")
    partners = []
    for level in range(levels):
        if level < col_bits:
            partners.append((row, flipped(col, 1 << level)))
        else:
            partners.append((flipped(row, 1 << (level - col_bits)), col))

    barrier = pltpu.get_barrier_semaphore()
    for partner in partners:
        pl.semaphore_signal(
            barrier, inc=1, device_id=partner, device_id_type=pl.DeviceIdType.MESH
        )

    loads = [
        pltpu.make_async_copy(source, target, load_sem.at[i])
        for i, (source, target) in enumerate(
            ((order_ref, order_v), (rhs_ref, rhs_v), (inv_ref, inv_v), (gen_ref, gen_v),
             (up_ref.at[0], up_v), (down_ref.at[0], down_v))
        )
    ]
    for load in loads:
        load.start()

    loads[0].wait()
    block = 128
    for start in range(0, bins, block):
        index = lax.broadcasted_iota(jnp.int32, (block, bins), 0) + start
        hit = index == order_v[...]
        place[start : start + block, :] = jnp.where(hit, 1.0, 0.0).astype(bf16)

    pl.semaphore_wait(barrier, levels)

    far = pltpu.make_async_remote_copy(
        src_ref=down_ref.at[0, levels - 1],
        dst_ref=far_v,
        send_sem=far_sem.at[0],
        recv_sem=far_sem.at[1],
        device_id=partners[levels - 1],
        device_id_type=pl.DeviceIdType.MESH,
    )
    far.start()

    events = list(range(levels)) + list(reversed(range(levels - 1)))
    copies = {}

    def rows(c):
        return slice(c * piece, (c + 1) * piece)

    def start(event, c, value):
        send[event, rows(c), :] = value
        copy = pltpu.make_async_remote_copy(
            src_ref=send.at[event, pl.ds(c * piece, piece)],
            dst_ref=recv.at[event, pl.ds(c * piece, piece)],
            send_sem=send_sem.at[event, c],
            recv_sem=recv_sem.at[event, c],
            device_id=partners[events[event]],
            device_id_type=pl.DeviceIdType.MESH,
        )
        copy.start()
        copies[event, c] = copy

    part = genes // leaf_parts
    loads[1].wait()
    rhs_t = rhs_v[...].T
    for h in range(leaf_parts):
        span = slice(h * part, (h + 1) * part)
        state = None
        for j in range(leaves):
            ordered = nn(rhs_t[span, :], place[:, j * leaf : (j + 1) * leaf]).astype(bf16)
            if h == 0 and j == 0:
                loads[2].wait()
            value = nt(ordered, inv_v[j])
            elim[j, span, :] = value
            if h == 0 and j == 0:
                loads[3].wait()
            own = nn(value.astype(bf16), gen_v[j])
            state = own if state is None else state + own
        states[0, span, :] = state
        if h == 0:
            loads[4].wait()
        term = nt(state.astype(bf16), up_v[0]).astype(bf16)
        for c in range(chunks // leaf_parts):
            start(0, h * (chunks // leaf_parts) + c, term[c * piece : (c + 1) * piece, :])

    last = 2 * levels - 2

    def go_up(level, c):
        copies[level - 1, c].wait_recv()
        state = send[level - 1, rows(c), :].astype(f32) + recv[level - 1, rows(c), :].astype(f32)
        states[level, rows(c), :] = state
        start(level, c, nt(state.astype(bf16), up_v[level]).astype(bf16))

    def go_down(event, c):
        level = events[event]
        copies[event - 1, c].wait_recv()
        came = recv[event - 1, rows(c), :].astype(f32)
        if event == levels:
            if c == 0:
                loads[5].wait()
                far.wait_recv()
            y = (send[event - 1, rows(c), :].astype(f32) + came).astype(bf16)
            coupled = nt(y, far_v[...]).astype(bf16).astype(f32)
            top = states[levels - 1, rows(c), :] + 0.5 * (coupled - nn(y, up_v[levels - 1]))
        else:
            top = states[level + 1, rows(c), :] + 0.5 * came
        y = top.astype(bf16)
        start(event, c, nt(y, down_v[level]).astype(bf16))
        states[level, rows(c), :] = states[level, rows(c), :] - 0.5 * nn(y, up_v[level])

    def finish(h):
        span = slice(h * part, (h + 1) * part)
        top = states[0, span, :] + 0.5 * recv[last, span, :].astype(f32)
        y = top.astype(bf16)
        for j in range(leaves):
            back = nt(y, gen_v[j]).astype(bf16)
            solved = elim[j, span, :] - nt(back, inv_v[j])
            flat[span, j * leaf : (j + 1) * leaf] = solved.astype(bf16)

    for slot in range(1, last + 1 + chunks):
        for c in range(chunks):
            event = slot - c
            if 0 < event < levels:
                go_up(event, c)
            elif levels <= event <= last:
                go_down(event, c)
            elif event == last + 1:
                copies[last, c].wait_recv()
                if (c + 1) * piece % part == 0:
                    finish(c * piece // part)
    out_ref[...] = nt(place[...], flat[...]).astype(bf16)

    for copy in copies.values():
        copy.wait_send()
    far.wait_send()


def on_device(
    rhs, order, leaf_inverse, leaf_column_generator, factor_up, downward_coupling_factors
):
    leaves, leaf, _ = leaf_inverse.shape
    rank = leaf_column_generator.shape[2]
    bins, genes = rhs.shape
    levels = factor_up.shape[1]
    col_bits = lax.axis_size("col").bit_length() - 1
    bf16, f32 = jnp.bfloat16, jnp.float32
    exchanges = 2 * levels - 1
    return pl.pallas_call(
        functools.partial(kernel, col_bits, CHUNKS, LEAF_PARTS),
        out_shape=jax.ShapeDtypeStruct((bins, genes), bf16),
        in_specs=[pl.BlockSpec(memory_space=pltpu.HBM)] * 6,
        out_specs=pl.BlockSpec(memory_space=pltpu.VMEM),
        scratch_shapes=[
            pltpu.VMEM((1, bins), jnp.int32),
            pltpu.VMEM((bins, genes), bf16),
            pltpu.VMEM((leaves, leaf, leaf), bf16),
            pltpu.VMEM((leaves, leaf, rank), bf16),
            pltpu.VMEM((levels, rank, rank), bf16),
            pltpu.VMEM((levels, rank, rank), bf16),
            pltpu.VMEM((rank, rank), bf16),
            pltpu.VMEM((bins, bins), bf16),
            pltpu.VMEM((leaves, genes, leaf), f32),
            pltpu.VMEM((levels, genes, rank), f32),
            pltpu.VMEM((genes, bins), bf16),
            pltpu.VMEM((exchanges, genes, rank), bf16),
            pltpu.VMEM((exchanges, genes, rank), bf16),
            pltpu.SemaphoreType.DMA((6,)),
            pltpu.SemaphoreType.DMA((exchanges, CHUNKS)),
            pltpu.SemaphoreType.DMA((exchanges, CHUNKS)),
            pltpu.SemaphoreType.DMA((2,)),
        ],
        compiler_params=pltpu.CompilerParams(
            collective_id=0, has_side_effects=True, vmem_limit_bytes=60 * 1024 * 1024
        ),
        cost_estimate=pl.CostEstimate(
            flops=2 * (2 * bins * bins * genes + 2 * bins * leaf * genes + 2 * bins * rank * genes
                       + 3 * levels * rank * rank * genes),
            bytes_accessed=4 * bins * genes + 2 * leaves * leaf * (leaf + rank)
            + 4 * levels * rank * rank,
            transcendentals=0,
        ),
    )(order, rhs, leaf_inverse, leaf_column_generator, factor_up, downward_coupling_factors)


def solution(mesh):
    in_specs = (
        P(("row", "col"), None),
        P(("row", "col"), None),
        P(("row", "col"), None, None),
        P(("row", "col"), None, None),
        P(("row", "col"), None, None, None),
        P(("row", "col"), None, None, None),
    )
    out_specs = P(("row", "col"), None)
    return jax.shard_map(
        on_device, mesh=mesh, in_specs=in_specs, out_specs=out_specs, check_vma=False
    )
```

```python
import functools

import jax
import jax.numpy as jnp
from jax import lax
from jax.experimental import pallas as pl
from jax.experimental.pallas import tpu as pltpu
from jax.sharding import PartitionSpec as P

CHUNKS = 2
LEAF_PARTS = 2


def nn(a, b):
    return lax.dot_general(a, b, (((1,), (0,)), ((), ())), preferred_element_type=jnp.float32)


def nt(a, b):
    return lax.dot_general(a, b, (((1,), (1,)), ((), ())), preferred_element_type=jnp.float32)


def flipped(index, bit):
    return index + bit * (1 - 2 * lax.rem(lax.div(index, bit), 2))


def kernel(
    col_bits,
    chunks,
    leaf_parts,
    order_ref,
    rhs_ref,
    inv_ref,
    gen_ref,
    up_ref,
    down_ref,
    out_ref,
    order_v,
    rhs_v,
    inv_v,
    gen_v,
    up_v,
    down_v,
    far_v,
    place,
    elim,
    states,
    flat,
    ys,
    send,
    recv,
    load_sem,
    send_sem,
    recv_sem,
    far_sem,
):
    bf16, f32 = jnp.bfloat16, jnp.float32
    levels = up_v.shape[0]
    leaves, leaf, _ = inv_v.shape
    bins, genes = rhs_v.shape
    piece = genes // chunks
    row, col = lax.axis_index("row"), lax.axis_index("col")
    partners = []
    for level in range(levels):
        if level < col_bits:
            partners.append((row, flipped(col, 1 << level)))
        else:
            partners.append((flipped(row, 1 << (level - col_bits)), col))

    barrier = pltpu.get_barrier_semaphore()
    for partner in partners:
        pl.semaphore_signal(
            barrier, inc=1, device_id=partner, device_id_type=pl.DeviceIdType.MESH
        )

    loads = [
        pltpu.make_async_copy(source, target, load_sem.at[i])
        for i, (source, target) in enumerate(
            ((order_ref, order_v), (rhs_ref, rhs_v), (inv_ref, inv_v), (gen_ref, gen_v),
             (up_ref.at[0], up_v), (down_ref.at[0], down_v))
        )
    ]
    for load in loads:
        load.start()

    loads[0].wait()
    block = 128
    for start in range(0, bins, block):
        index = lax.broadcasted_iota(jnp.int32, (block, bins), 0) + start
        hit = index == order_v[...]
        place[start : start + block, :] = jnp.where(hit, 1.0, 0.0).astype(bf16)

    pl.semaphore_wait(barrier, levels)

    far = pltpu.make_async_remote_copy(
        src_ref=down_ref.at[0, levels - 1],
        dst_ref=far_v,
        send_sem=far_sem.at[0],
        recv_sem=far_sem.at[1],
        device_id=partners[levels - 1],
        device_id_type=pl.DeviceIdType.MESH,
    )
    far.start()

    events = list(range(levels)) + list(reversed(range(levels - 1)))
    copies = {}

    def rows(c):
        return slice(c * piece, (c + 1) * piece)

    def start(event, c, value):
        send[event, rows(c), :] = value
        copy = pltpu.make_async_remote_copy(
            src_ref=send.at[event, pl.ds(c * piece, piece)],
            dst_ref=recv.at[event, pl.ds(c * piece, piece)],
            send_sem=send_sem.at[event, c],
            recv_sem=recv_sem.at[event, c],
            device_id=partners[events[event]],
            device_id_type=pl.DeviceIdType.MESH,
        )
        copy.start()
        copies[event, c] = copy

    part = genes // leaf_parts
    loads[1].wait()
    rhs_t = rhs_v[...].T
    for h in range(leaf_parts):
        span = slice(h * part, (h + 1) * part)
        state = None
        for j in range(leaves):
            ordered = nn(rhs_t[span, :], place[:, j * leaf : (j + 1) * leaf]).astype(bf16)
            if h == 0 and j == 0:
                loads[2].wait()
            value = nt(ordered, inv_v[j])
            elim[j, span, :] = value
            if h == 0 and j == 0:
                loads[3].wait()
            own = nn(value.astype(bf16), gen_v[j])
            state = own if state is None else state + own
        states[0, span, :] = state
        if h == 0:
            loads[4].wait()
        term = nt(state.astype(bf16), up_v[0]).astype(bf16)
        for c in range(chunks // leaf_parts):
            start(0, h * (chunks // leaf_parts) + c, term[c * piece : (c + 1) * piece, :])

    for level in range(1, levels):
        for c in range(chunks):
            copies[level - 1, c].wait_recv()
            state = send[level - 1, rows(c), :].astype(f32) + recv[level - 1, rows(c), :].astype(
                f32
            )
            states[level, rows(c), :] = state
            start(level, c, nt(state.astype(bf16), up_v[level]).astype(bf16))

    for event in range(levels, 2 * levels - 1):
        level = events[event]
        for c in range(chunks):
            copies[event - 1, c].wait_recv()
            came = recv[event - 1, rows(c), :].astype(f32)
            if event == levels:
                if c == 0:
                    loads[5].wait()
                    far.wait_recv()
                y = (send[event - 1, rows(c), :].astype(f32) + came).astype(bf16)
                coupled = nt(y, far_v[...]).astype(bf16).astype(f32)
                top = states[levels - 1, rows(c), :] + 0.5 * (coupled - nn(y, up_v[levels - 1]))
            else:
                top = states[level + 1, rows(c), :] + 0.5 * came
            y = top.astype(bf16)
            start(event, c, nt(y, down_v[level]).astype(bf16))
            ys[rows(c), :] = y
        states[level] = states[level] - 0.5 * nn(ys[...], up_v[level])

    last = 2 * levels - 2
    for h in range(leaf_parts):
        span = slice(h * part, (h + 1) * part)
        for c in range(h * (chunks // leaf_parts), (h + 1) * (chunks // leaf_parts)):
            copies[last, c].wait_recv()
        top = states[0, span, :] + 0.5 * recv[last, span, :].astype(f32)
        y = top.astype(bf16)
        for j in range(leaves):
            back = nt(y, gen_v[j]).astype(bf16)
            solved = elim[j, span, :] - nt(back, inv_v[j])
            flat[span, j * leaf : (j + 1) * leaf] = solved.astype(bf16)
    out_ref[...] = nt(place[...], flat[...]).astype(bf16)

    for copy in copies.values():
        copy.wait_send()
    far.wait_send()


def on_device(
    rhs, order, leaf_inverse, leaf_column_generator, factor_up, downward_coupling_factors
):
    leaves, leaf, _ = leaf_inverse.shape
    rank = leaf_column_generator.shape[2]
    bins, genes = rhs.shape
    levels = factor_up.shape[1]
    col_bits = lax.axis_size("col").bit_length() - 1
    bf16, f32 = jnp.bfloat16, jnp.float32
    exchanges = 2 * levels - 1
    return pl.pallas_call(
        functools.partial(kernel, col_bits, CHUNKS, LEAF_PARTS),
        out_shape=jax.ShapeDtypeStruct((bins, genes), bf16),
        in_specs=[pl.BlockSpec(memory_space=pltpu.HBM)] * 6,
        out_specs=pl.BlockSpec(memory_space=pltpu.VMEM),
        scratch_shapes=[
            pltpu.VMEM((1, bins), jnp.int32),
            pltpu.VMEM((bins, genes), bf16),
            pltpu.VMEM((leaves, leaf, leaf), bf16),
            pltpu.VMEM((leaves, leaf, rank), bf16),
            pltpu.VMEM((levels, rank, rank), bf16),
            pltpu.VMEM((levels, rank, rank), bf16),
            pltpu.VMEM((rank, rank), bf16),
            pltpu.VMEM((bins, bins), bf16),
            pltpu.VMEM((leaves, genes, leaf), f32),
            pltpu.VMEM((levels, genes, rank), f32),
            pltpu.VMEM((genes, bins), bf16),
            pltpu.VMEM((genes, rank), bf16),
            pltpu.VMEM((exchanges, genes, rank), bf16),
            pltpu.VMEM((exchanges, genes, rank), bf16),
            pltpu.SemaphoreType.DMA((6,)),
            pltpu.SemaphoreType.DMA((exchanges, CHUNKS)),
            pltpu.SemaphoreType.DMA((exchanges, CHUNKS)),
            pltpu.SemaphoreType.DMA((2,)),
        ],
        compiler_params=pltpu.CompilerParams(
            collective_id=0, has_side_effects=True, vmem_limit_bytes=60 * 1024 * 1024
        ),
        cost_estimate=pl.CostEstimate(
            flops=2 * (2 * bins * bins * genes + 2 * bins * leaf * genes + 2 * bins * rank * genes
                       + 3 * levels * rank * rank * genes),
            bytes_accessed=4 * bins * genes + 2 * leaves * leaf * (leaf + rank)
            + 4 * levels * rank * rank,
            transcendentals=0,
        ),
    )(order, rhs, leaf_inverse, leaf_column_generator, factor_up, downward_coupling_factors)


def solution(mesh):
    in_specs = (
        P(("row", "col"), None),
        P(("row", "col"), None),
        P(("row", "col"), None, None),
        P(("row", "col"), None, None),
        P(("row", "col"), None, None, None),
        P(("row", "col"), None, None, None),
    )
    out_specs = P(("row", "col"), None)
    return jax.shard_map(
        on_device, mesh=mesh, in_specs=in_specs, out_specs=out_specs, check_vma=False
    )
```
